1024 devices in a mesh: grp: 16 (over z_lo), dp: 64 (over y, z_hi, x, core).
Axes of the slice: x: 4, y: 4, z: 32 (z_hi: 2, z_lo: 16; z = z_hi * 16 + z_lo), core: 2. Of those that a mesh axis runs over, the one named last changes fastest.
Arguments:
- query_emb: bfloat16 [131072, 768], P(('grp', 'dp')), may hold values from -2 to 2
- passage_emb: bfloat16 [16384, 768], P(('grp', 'dp')), may hold values from -2 to 2
- positives: int32 [131072], P(('grp', 'dp')), may hold values from 0 to 1023
- hard_lists: int32 [16, 64, 4], P('grp', 'dp'), may hold values from 0 to 15, as said below
- hard_counts: int32 [16, 64], P('grp', 'dp'), may hold values from 1 to 4
Outputs:
- question_derivative: bfloat16 [131072, 768], P(('grp', 'dp'))
- passage_grad: bfloat16 [16384, 768], P(('grp', 'dp'))
- losses: float32 [131072], P(('grp', 'dp'))
The draws below stay inside these ranges and needn't reach their ends.
Inputs may be any that keep to these rules, and one draw needn't show every extreme that they name: `hard_lists`: the entries of one device's list are distinct and never its own group.
All inputs are finite; a program needn't handle non-finite values.
Results may differ from the reference program's by a relative error of at most 0.0055.
Values may be sent and summed in bfloat16 or wider, within the bound.
A program may use at most 32 MiB of HBM per device.

```python
import jax
import jax.numpy as jnp
from jax import lax

D = 768
Q_DEV = 128
P_DEV = 16
HN = 4
PG = 1024
NQ = 131072
NP = 16384
N_GRP = 16
N_DP = 64


def passage_rows(key, boost):
    base = jax.random.normal(jax.random.fold_in(key, 11), (NP, D), jnp.float32)
    row_ids = jnp.arange(NP)
    marked = (row_ids // 2 % 5 == 0) & (boost > 1.0)
    leader = jnp.repeat(base.reshape(NP // 2, 2, D)[:, 0], 2, axis=0)
    strong = leader
    drawn = base
    return jnp.clip(0.06 * jnp.where(marked[:, None], strong, drawn), -2.0, 2.0)


def query_rows(key, boost):
    passages = passage_rows(key, boost)
    key = jax.random.fold_in(key, 2)
    base = jax.random.normal(jax.random.fold_in(key, 21), (NQ, D), jnp.float32)
    factor = jax.random.uniform(jax.random.fold_in(key, 23), (NQ, 1), jnp.float32, 0.6, 1.0)
    row_ids = jnp.arange(NQ)
    group_of = row_ids // (Q_DEV * N_DP)
    target = group_of * PG + 10 * (row_ids % (PG // 10))
    aligned = (row_ids % 37 == 0) & (boost > 1.0)
    drawn = 0.06 * base
    return jnp.clip(jnp.where(aligned[:, None], factor * passages[target], drawn), -2.0, 2.0)


def draw_passage_emb(key, part):
    return passage_rows(key, 1.0).astype(jnp.bfloat16)


def draw_query_emb(key, part):
    return query_rows(key, 1.0).astype(jnp.bfloat16)


def draw_hard_lists(key, part):
    key = jax.random.fold_in(key, 5)
    keys = jax.random.split(key, N_GRP * N_DP)
    orders = jax.vmap(lambda one_key: jax.random.permutation(one_key, N_GRP - 1))(keys)[:, :HN]
    owners = (jnp.arange(N_GRP * N_DP) // N_DP)[:, None]
    groups = orders + (orders >= owners).astype(jnp.int32)
    return groups.reshape(N_GRP, N_DP, HN).astype(jnp.int32)


def draw_hard_counts(key, part):
    key = jax.random.fold_in(key, 7)
    counts = jax.random.randint(key, (N_GRP, N_DP), 1, HN + 1)
    counts = counts.at[0, 0].set(HN)
    counts = counts.at[N_GRP - 1, N_DP - 1].set(1)
    return counts.astype(jnp.int32)


def with_ends(values, rng, low, top_value):
    longest = values.shape.index(max(values.shape))
    spots = []
    for shift in (0, 1):
        where = [jax.random.randint(jax.random.fold_in(rng, axis), (), 0, length) for axis, length in enumerate(values.shape)]
        where[longest] = (where[longest] + shift) % values.shape[longest]
        spots.append(tuple(where))
    return values.at[spots[0]].set(low).at[spots[1]].set(top_value)


def setup_inputs(seed: int = 0) -> dict:
    streams_of = jax.random.split(jax.random.key(seed), 6)
    query_emb = draw_query_emb(jax.random.fold_in(streams_of[5], 71), 0)
    passage_emb = draw_passage_emb(jax.random.fold_in(streams_of[5], 71), 0)
    positives = with_ends(jax.random.randint(streams_of[2], (NQ,), 0, PG), jax.random.fold_in(streams_of[2], 1), 0, PG - 1).astype(jnp.int32)
    hard_lists = draw_hard_lists(jax.random.fold_in(streams_of[5], 71), 0)
    hard_counts = draw_hard_counts(jax.random.fold_in(streams_of[5], 71), 0)
    return {"query_emb": query_emb, "passage_emb": passage_emb, "positives": positives, "hard_lists": hard_lists, "hard_counts": hard_counts}


inverse_softmax_scale = 20.0
dead_score = -1e30


def device_terms(question_matrix, positive, batch_passage_half, mined_passage_half, live_rows):
    batch_passage_logit = jnp.dot(question_matrix, batch_passage_half.T, preferred_element_type=jnp.float32) * inverse_softmax_scale
    mined_passage_logit = jnp.dot(question_matrix, mined_passage_half.T, preferred_element_type=jnp.float32) * inverse_softmax_scale
    mined_passage_logit = jnp.where(live_rows[None, :], mined_passage_logit, dead_score)
    row_max = jnp.maximum(jnp.max(batch_passage_logit, axis=1), jnp.max(mined_passage_logit, axis=1))
    total = jnp.sum(jnp.exp(batch_passage_logit - row_max[:, None]), axis=1) + jnp.sum(jnp.exp(mined_passage_logit - row_max[:, None]), axis=1)
    log_total = row_max + jnp.log(total)
    column_ids = jnp.arange(batch_passage_half.shape[0], dtype=jnp.int32)
    hit_mask = column_ids[None, :] == positive[:, None]
    pos_score = jnp.sum(jnp.where(hit_mask, batch_passage_logit, 0.0), axis=1)
    losses = log_total - pos_score
    batch_passage_derivative = (jnp.exp(batch_passage_logit - log_total[:, None]) - hit_mask.astype(jnp.float32)).astype(jnp.bfloat16)
    mined_passage_derivative = jnp.exp(mined_passage_logit - log_total[:, None]).astype(jnp.bfloat16)
    question_derivative = (jnp.dot(batch_passage_derivative, batch_passage_half, preferred_element_type=jnp.float32) + jnp.dot(mined_passage_derivative, mined_passage_half, preferred_element_type=jnp.float32)) * inverse_softmax_scale
    batch_passage_addend = jnp.dot(batch_passage_derivative.T, question_matrix, preferred_element_type=jnp.float32) * inverse_softmax_scale
    mined_passage_addend = jnp.dot(mined_passage_derivative.T, question_matrix, preferred_element_type=jnp.float32) * inverse_softmax_scale
    return question_derivative.astype(jnp.bfloat16), losses, batch_passage_addend, mined_passage_addend


def reference(query_emb, passage_emb, positives, hard_lists, hard_counts):
    blocks = passage_emb.reshape(N_GRP, N_DP, P_DEV, D)
    group_ids = jnp.arange(N_GRP, dtype=jnp.int32)
    slot_ids = jnp.arange(HN, dtype=jnp.int32)

    def step(carry, index):
        group = index // N_DP
        column = index % N_DP
        question_matrix = lax.dynamic_slice_in_dim(query_emb, (index * Q_DEV).astype(jnp.int32), Q_DEV, 0)
        positive = lax.dynamic_slice_in_dim(positives, (index * Q_DEV).astype(jnp.int32), Q_DEV, 0)
        batch_passage_half = lax.dynamic_index_in_dim(blocks, group, 0, keepdims=False).reshape(PG, D)
        mined_passage_half = lax.dynamic_index_in_dim(blocks, column, 1, keepdims=False).reshape(N_GRP * P_DEV, D)
        chosen = hard_lists[group, column]
        live_slots = slot_ids < hard_counts[group, column]
        listed = jnp.any((chosen[:, None] == group_ids[None, :]) & live_slots[:, None], axis=0)
        live_rows = jnp.repeat(listed, P_DEV)
        question_derivative, losses, batch_passage_addend, mined_passage_addend = device_terms(question_matrix, positive, batch_passage_half, mined_passage_half, live_rows)
        carry = carry.at[group].add(batch_passage_addend.reshape(N_DP, P_DEV, D))
        carry = carry.at[:, column].add(mined_passage_addend.reshape(N_GRP, P_DEV, D))
        return carry, (question_derivative, losses)

    start = jnp.zeros((N_GRP, N_DP, P_DEV, D), jnp.float32)
    summed, (question_derivative, losses) = lax.scan(step, start, jnp.arange(N_GRP * N_DP, dtype=jnp.int32))
    return question_derivative.reshape(NQ, D), summed.reshape(NP, D).astype(jnp.bfloat16), losses.reshape(NQ)
```

```python
import jax
import jax.numpy as jnp
from jax import lax
from jax.experimental import pallas as pl
from jax.experimental.pallas import tpu as pltpu
from jax.sharding import PartitionSpec as P

MESH = pl.DeviceIdType.MESH
SCALE = 20.0
DEAD = -1e30
GROUPS = 16
ROWS = 16
QUERIES = 128
WIDTH = 768
HUBS = (-2, -1, 1, 2)
NEAR = (-1, 1, -2, 2, -3, 3, -4, 4, -5, 5)
SHIFTS = tuple((dy, dx) for dy in range(4) for dx in range(4) if (dy, dx) != (0, 0))


def inside(h):
    return (h >= 0) & (h < GROUPS)


def is_leaf(k, e, hub):
    ok = inside(hub - 5 * k) & inside(hub + e)
    if abs(e) <= 2:
        return ok
    if (e > 0 and k < 0) or (e < 0 and k > 0):
        return None
    if abs(k) == 2:
        return ok
    return ok & ((hub >= 11) if e > 0 else (hub <= 4))


def is_relay(k, hub):
    if k == 2:
        return hub >= 10
    if k == -2:
        return hub <= 5
    if k == 1:
        return (hub == 13) | (hub == 14)
    return (hub == 1) | (hub == 2)


def rows_of(index):
    return pl.ds(pl.multiple_of(index * ROWS, ROWS), ROWS)


def score(a, b):
    return SCALE * lax.dot_general(
        a, b, (((1,), (1,)), ((), ())), preferred_element_type=jnp.float32
    )


def over_rows(a, b):
    return lax.dot_general(a, b, (((0,), (0,)), ((), ())), preferred_element_type=jnp.float32)


def dot(a, b):
    return jnp.dot(a, b, preferred_element_type=jnp.float32)


def kernel(
    q_in, p_in, pos_in, lists, counts,
    dq_out, dp_out, loss_out,
    q_buf, pos_own, pos_sib, p_buf, o_buf, s_buf, so_buf, g_buf, go_buf,
    st_mine, st_sib, dq_mine, dq_send, dq_sib,
    d_buf, r_buf, do_buf, leaf_buf, hub_buf, sum_buf, relay_buf, far_buf, acc,
    loc_sem, line_recv, hub_send, leaf_send, relay_send, far_recv, plane_send, plane_recv,
    sib_send, sib_recv, d_send, d_recv, leaf_send2, leaf_recv2, hub_send2, hub_recv2,
    sum_send, relay_recv2, relay_send2, far_recv2,
):
    g = lax.axis_index("grp")
    d = lax.axis_index("dp")
    y, zh, x, c = d // 16, (d // 8) % 2, (d // 2) % 4, d % 2

    def at(yy, zz, xx, cc):
        return ((yy * 2 + zz) * 4 + xx) * 2 + cc

    sib = (g, at(y, zh, x, 1 - c))
    plane = [(g, at((y + dy) % 4, zh, (x + dx) % 4, c)) for dy, dx in SHIFTS]
    far_dp = at(y, 1 - zh, x, c)
    my_slot = y * 4 + x
    my_k = jnp.where(g <= 5, 2, jnp.where(g <= 7, -1, jnp.where(g <= 9, 1, -2)))
    my_relay = g + 5 * my_k

    def copy(src, dst, send, recv, dev):
        return pltpu.make_async_remote_copy(
            src_ref=src, dst_ref=dst, send_sem=send, recv_sem=recv,
            device_id=dev, device_id_type=MESH,
        )

    def received(dst, sem):
        copy(dst, dst, sem, sem, sib).wait_recv()

    def sent(src, sem):
        copy(src, src, sem, sem, sib).wait_send()

    barrier = pltpu.get_barrier_semaphore()

    def tell(dev):
        pl.semaphore_signal(barrier, inc=1, device_id=dev, device_id_type=MESH)

    expected = jnp.int32(1 + len(SHIFTS))
    for o in (-10, 10, -5, 5, -4, 4, -3, 3, -2, 2, -1, 1):
        ok = inside(g + o)
        pl.when(ok)(lambda o=o: tell((g + o, d)))
        expected = expected + ok.astype(jnp.int32)
    tell((my_relay, far_dp))
    for k in HUBS:
        expected = expected + is_relay(k, g).astype(jnp.int32)
    for dev in plane:
        tell(dev)
    tell(sib)

    own = p_buf.at[rows_of(my_slot)]
    local = [
        pltpu.make_async_copy(p_in, own, loc_sem.at[0]),
        pltpu.make_async_copy(p_in, o_buf.at[rows_of(g)], loc_sem.at[1]),
        pltpu.make_async_copy(q_in, q_buf.at[pl.ds(0, QUERIES)], loc_sem.at[2]),
        pltpu.make_async_copy(pos_in, pos_own, loc_sem.at[3]),
    ]
    for cp in local:
        cp.start()
    for cp in local:
        cp.wait()
    pl.semaphore_wait(barrier, expected)

    def hub_copy(i, k):
        return copy(own, o_buf.at[rows_of(g)], hub_send.at[i], line_recv.at[g], (g + 5 * k, d))

    def leaf_copy(kk, k, j, e):
        block = o_buf.at[rows_of(g - 5 * k)]
        return copy(block, block, leaf_send.at[kk, j], line_recv.at[g - 5 * k], (g + e, d))

    def leaf_starts(kk, k):
        for j, e in enumerate(NEAR):
            ok = is_leaf(k, e, g)
            if ok is not None:
                pl.when(ok)(lambda kk=kk, k=k, j=j, e=e: leaf_copy(kk, k, j, e).start())

    def far_copy(i, k):
        return copy(
            o_buf.at[rows_of(g - 5 * k)], p_buf.at[rows_of(16 + my_slot)],
            relay_send.at[i], far_recv.at[0], (g - 5 * k, far_dp),
        )

    def plane_copy(part, i):
        block = p_buf.at[rows_of(part * 16 + my_slot)]
        return copy(block, block, plane_send.at[part, i], plane_recv.at[part, i], plane[i])

    for i, k in ((0, -2), (3, 2), (1, -1), (2, 1)):
        pl.when(inside(g + 5 * k))(lambda i=i, k=k: hub_copy(i, k).start())
    for i in range(15):
        plane_copy(0, i).start()
    leaf_starts(2, 0)
    q_copy = copy(
        q_buf.at[pl.ds(0, QUERIES)], q_buf.at[pl.ds(QUERIES, QUERIES)],
        sib_send.at[0], sib_recv.at[0], sib,
    )
    pos_copy = copy(pos_own, pos_sib, sib_send.at[1], sib_recv.at[1], sib)
    q_copy.start()
    pos_copy.start()

    for i, k, kk in ((1, -1, 1), (2, 1, 3), (0, -2, 0), (3, 2, 4)):

        @pl.when(inside(g - 5 * k))
        def _(i=i, k=k, kk=kk):
            received(o_buf.at[rows_of(g - 5 * k)], line_recv.at[g - 5 * k])
            pl.when(is_relay(k, g))(lambda: far_copy(i, k).start())
            leaf_starts(kk, k)

    q_copy.wait_recv()
    pos_copy.wait_recv()
    for i in range(15):
        plane_copy(0, i).wait_recv()
    s_buf[0:256] = score(p_buf[0:256], q_buf[...])

    received(p_buf.at[rows_of(16 + my_slot)], far_recv.at[0])
    for i in range(15):
        plane_copy(1, i).start()

    for o in range(1, GROUPS):
        h = (g + o) % GROUPS
        direct = False
        for k in HUBS:
            direct = direct | (h == g - 5 * k)
        pl.when(jnp.logical_not(direct))(
            lambda h=h: received(o_buf.at[rows_of(h)], line_recv.at[h])
        )
    row_group = lax.broadcasted_iota(jnp.int32, (GROUPS * ROWS, QUERIES), 0) >> 4
    live = jnp.zeros((GROUPS * ROWS, QUERIES), jnp.bool_)
    for i in range(4):
        entry = jnp.where(i < counts[0, 0], lists[0, i], -1)
        live = live | (row_group == entry)
    outer = jnp.where(live, score(o_buf[...], q_buf[0:QUERIES]), DEAD)
    so_buf[...] = outer
    outer_max = jnp.max(outer, axis=0, keepdims=True)
    outer_sum = jnp.sum(jnp.exp(outer - outer_max), axis=0, keepdims=True)

    for i in range(15):
        plane_copy(1, i).wait_recv()
    s_buf[256:512] = score(p_buf[256:512], q_buf[...])

    pos = jnp.concatenate([pos_own[...], pos_sib[...]], axis=1)

    def hits(part):
        i = lax.broadcasted_iota(jnp.int32, (256, 2 * QUERIES), 0)
        zz = zh + part - 2 * zh * part
        column = ((i >> 6) << 8) + zz * 128 + (((i >> 4) & 3) << 5) + c * 16 + (i & 15)
        return column == pos

    s0, s1 = s_buf[0:256], s_buf[256:512]
    top = jnp.maximum(jnp.max(s0, axis=0, keepdims=True), jnp.max(s1, axis=0, keepdims=True))
    total = jnp.sum(jnp.exp(s0 - top), axis=0, keepdims=True) + jnp.sum(
        jnp.exp(s1 - top), axis=0, keepdims=True
    )
    picked = jnp.sum(jnp.where(hits(0), s0, 0.0), axis=0, keepdims=True) + jnp.sum(
        jnp.where(hits(1), s1, 0.0), axis=0, keepdims=True
    )
    own_top = jnp.maximum(top[:, :QUERIES], outer_max)
    own_total = total[:, :QUERIES] * jnp.exp(top[:, :QUERIES] - own_top) + outer_sum * jnp.exp(
        outer_max - own_top
    )
    top = jnp.concatenate([own_top, top[:, QUERIES:]], axis=1)
    total = jnp.concatenate([own_total, total[:, QUERIES:]], axis=1)
    st_mine[0:1] = top
    st_mine[1:2] = total
    st_mine[2:3] = picked
    st_mine[3:8] = jnp.zeros((5, 2 * QUERIES), jnp.float32)
    st_copy = copy(st_mine, st_sib, sib_send.at[2], sib_recv.at[2], sib)
    st_copy.start()

    for i, k in enumerate(HUBS):
        pl.when(inside(g + 5 * k))(lambda i=i, k=k: hub_copy(i, k).wait_send())

        @pl.when(inside(g - 5 * k))
        def _(i=i, k=k):
            pl.when(is_relay(k, g))(lambda: far_copy(i, k).wait_send())

    for kk in range(5):
        for j, e in enumerate(NEAR):
            ok = is_leaf(kk - 2, e, g)
            if ok is not None:
                pl.when(ok)(lambda kk=kk, j=j, e=e: leaf_copy(kk, kk - 2, j, e).wait_send())
    for i in range(15):
        plane_copy(0, i).wait_send()
        plane_copy(1, i).wait_send()
    q_copy.wait_send()
    pos_copy.wait_send()

    st_copy.wait()
    swapped = jnp.concatenate([st_sib[:, QUERIES:], st_sib[:, :QUERIES]], axis=1)
    both_top = jnp.maximum(top, swapped[0:1])
    both = total * jnp.exp(top - both_top) + swapped[1:2] * jnp.exp(swapped[0:1] - both_top)
    log_total = both_top + jnp.log(both)
    loss_out[...] = (log_total - (picked + swapped[2:3]))[:, :QUERIES]

    def part_grad(part):
        a = jnp.exp(s_buf[part * 256 : part * 256 + 256] - log_total)
        a = (a - hits(part).astype(jnp.float32)).astype(jnp.bfloat16)
        g_buf[part * 256 : part * 256 + 256] = a
        d_buf[part * 256 : part * 256 + 256] = (SCALE * dot(a, q_buf[...])).astype(jnp.bfloat16)

    def d_copy(part, i):
        dy, dx = SHIFTS[i]
        slot = part * 16 + ((y + dy) % 4) * 4 + (x + dx) % 4
        return copy(
            d_buf.at[rows_of(slot)], r_buf.at[part, i], d_send.at[part, i], d_recv.at[part, i],
            plane[i],
        )

    def leaf_back(kk, k, j, e):
        return copy(
            do_buf.at[rows_of(g - e - 5 * k)], leaf_buf.at[kk, j], leaf_send2.at[kk, j],
            leaf_recv2.at[kk, j], (g - e, d),
        )

    part_grad(1)
    for i in range(15):
        d_copy(1, i).start()
    a = jnp.where(live, jnp.exp(so_buf[...] - log_total[:, :QUERIES]), 0.0).astype(jnp.bfloat16)
    go_buf[...] = a
    do_buf[...] = (SCALE * dot(a, q_buf[0:QUERIES])).astype(jnp.bfloat16)
    for kk in (0, 4, 1, 3, 2):
        for j, e in enumerate(NEAR):
            ok = is_leaf(kk - 2, e, g - e)
            if ok is not None:
                ok = ok & inside(g - e)
                pl.when(ok)(lambda kk=kk, j=j, e=e: leaf_back(kk, kk - 2, j, e).start())
    part_grad(0)
    for i in range(15):
        d_copy(0, i).start()

    dq_send[...] = over_rows(g_buf[:, QUERIES:], p_buf[...])
    dq_copy = copy(dq_send, dq_sib, sib_send.at[3], sib_recv.at[3], sib)
    dq_copy.start()

    def add_leaves(kk, k):
        for j, e in enumerate(NEAR):
            ok = is_leaf(k, e, g)
            if ok is not None:

                @pl.when(ok)
                def _(kk=kk, j=j):
                    received(leaf_buf.at[kk, j], leaf_recv2.at[kk, j])
                    acc[...] += leaf_buf[kk, j].astype(jnp.float32)

    def hub_back(i, k):
        return copy(
            sum_buf.at[i], hub_buf.at[i], hub_send2.at[i], hub_recv2.at[i], (g - 5 * k, d)
        )

    def add_hub(i, k, kk):
        @pl.when(inside(g - 5 * k))
        def _():
            acc[...] = do_buf[rows_of(g - 5 * k)].astype(jnp.float32)
            add_leaves(kk, k)
            sum_buf[i] = acc[...].astype(jnp.bfloat16)
            hub_back(i, k).start()

    add_hub(0, -2, 0)
    add_hub(3, 2, 4)

    total_far = d_buf[rows_of(16 + my_slot)].astype(jnp.float32)
    for i in range(15):
        d_copy(1, i).wait_recv()
        total_far = total_far + r_buf[1, i].astype(jnp.float32)
    sum_buf[4] = total_far.astype(jnp.bfloat16)
    for i, k in enumerate(HUBS):

        @pl.when(my_k == k)
        def _(i=i, k=k):
            copy(
                sum_buf.at[4], relay_buf.at[i], sum_send.at[0], relay_recv2.at[i], (g + 5 * k, d)
            ).start()

    add_hub(1, -1, 1)
    add_hub(2, 1, 3)

    def relay_back(i, k):
        return copy(
            relay_buf.at[i], far_buf, relay_send2.at[i], far_recv2.at[0], (g - 5 * k, far_dp)
        )

    for i, k in enumerate(HUBS):

        @pl.when(is_relay(k, g))
        def _(i=i, k=k):
            received(relay_buf.at[i], relay_recv2.at[i])
            relay_back(i, k).start()

    dq_mine[...] = over_rows(g_buf[:, :QUERIES], p_buf[...]) + over_rows(go_buf[...], o_buf[...])
    dq_copy.wait_recv()
    dq_out[...] = (SCALE * (dq_mine[...] + dq_sib[...])).astype(jnp.bfloat16)

    acc[...] = d_buf[rows_of(my_slot)].astype(jnp.float32) + do_buf[rows_of(g)].astype(jnp.float32)
    for i in range(15):
        d_copy(0, i).wait_recv()
        acc[...] += r_buf[0, i].astype(jnp.float32)
    add_leaves(2, 0)
    for i, k in enumerate(HUBS):

        @pl.when(inside(g + 5 * k))
        def _(i=i, k=k):
            received(hub_buf.at[i], hub_recv2.at[i])
            acc[...] += hub_buf[i].astype(jnp.float32)

    received(far_buf, far_recv2.at[0])
    dp_out[...] = (acc[...] + far_buf[...].astype(jnp.float32)).astype(jnp.bfloat16)

    for i in range(15):
        d_copy(0, i).wait_send()
        d_copy(1, i).wait_send()
    for kk in range(5):
        for j, e in enumerate(NEAR):
            ok = is_leaf(kk - 2, e, g - e)
            if ok is not None:
                ok = ok & inside(g - e)
                pl.when(ok)(lambda kk=kk, j=j, e=e: leaf_back(kk, kk - 2, j, e).wait_send())
    for i, k in enumerate(HUBS):
        pl.when(inside(g - 5 * k))(lambda i=i, k=k: hub_back(i, k).wait_send())
        pl.when(is_relay(k, g))(lambda i=i, k=k: relay_back(i, k).wait_send())
    sent(sum_buf.at[4], sum_send.at[0])
    dq_copy.wait_send()


def per_device(query_emb, passage_emb, positives, hard_lists, hard_counts):
    bf16, f32, i32 = jnp.bfloat16, jnp.float32, jnp.int32
    dma = pltpu.SemaphoreType.DMA
    block = (ROWS, WIDTH)
    anywhere = pl.BlockSpec(memory_space=pl.ANY)
    smem = pl.BlockSpec(memory_space=pltpu.SMEM)
    vmem = pl.BlockSpec(memory_space=pltpu.VMEM)
    dq, dp, loss = pl.pallas_call(
        kernel,
        out_shape=(
            jax.ShapeDtypeStruct((QUERIES, WIDTH), bf16),
            jax.ShapeDtypeStruct(block, bf16),
            jax.ShapeDtypeStruct((1, QUERIES), f32),
        ),
        in_specs=[anywhere, anywhere, anywhere, smem, smem],
        out_specs=(vmem, vmem, vmem),
        scratch_shapes=[
            pltpu.VMEM((2 * QUERIES, WIDTH), bf16),
            pltpu.VMEM((1, QUERIES), i32),
            pltpu.VMEM((1, QUERIES), i32),
            pltpu.VMEM((512, WIDTH), bf16),
            pltpu.VMEM((256, WIDTH), bf16),
            pltpu.VMEM((512, 2 * QUERIES), f32),
            pltpu.VMEM((256, QUERIES), f32),
            pltpu.VMEM((512, 2 * QUERIES), bf16),
            pltpu.VMEM((256, QUERIES), bf16),
            pltpu.VMEM((8, 2 * QUERIES), f32),
            pltpu.VMEM((8, 2 * QUERIES), f32),
            pltpu.VMEM((QUERIES, WIDTH), f32),
            pltpu.VMEM((QUERIES, WIDTH), f32),
            pltpu.VMEM((QUERIES, WIDTH), f32),
            pltpu.VMEM((512, WIDTH), bf16),
            pltpu.VMEM((2, 15) + block, bf16),
            pltpu.VMEM((256, WIDTH), bf16),
            pltpu.VMEM((5, 10) + block, bf16),
            pltpu.VMEM((4,) + block, bf16),
            pltpu.VMEM((5,) + block, bf16),
            pltpu.VMEM((4,) + block, bf16),
            pltpu.VMEM(block, bf16),
            pltpu.VMEM(block, f32),
            dma((4,)),
            dma((16,)),
            dma((4,)),
            dma((5, 10)),
            dma((4,)),
            dma((1,)),
            dma((2, 15)),
            dma((2, 15)),
            dma((4,)),
            dma((4,)),
            dma((2, 15)),
            dma((2, 15)),
            dma((5, 10)),
            dma((5, 10)),
            dma((4,)),
            dma((4,)),
            dma((1,)),
            dma((4,)),
            dma((4,)),
            dma((1,)),
        ],
        name="dual_encoder",
        compiler_params=pltpu.CompilerParams(
            collective_id=0, has_side_effects=True, vmem_limit_bytes=40 * 1024 * 1024
        ),
    )(
        query_emb, passage_emb, positives.reshape(1, QUERIES), hard_lists.reshape(1, 4),
        hard_counts,
    )
    return dq, dp, loss.reshape(QUERIES)


def solution(mesh):
    in_specs = (
        P(("grp", "dp"), None),
        P(("grp", "dp"), None),
        P(("grp", "dp")),
        P("grp", "dp", None),
        P("grp", "dp"),
    )
    out_specs = (P(("grp", "dp"), None), P(("grp", "dp"), None), P(("grp", "dp")))
    return jax.shard_map(
        per_device, mesh=mesh, in_specs=in_specs, out_specs=out_specs, check_vma=False
    )
```

```python
import jax
import jax.numpy as jnp
from jax import lax
from jax.experimental import pallas as pl
from jax.experimental.pallas import tpu as pltpu
from jax.sharding import PartitionSpec as P

MESH = pl.DeviceIdType.MESH
SCALE = 20.0
DEAD = -1e30
GROUPS = 16
ROWS = 16
QUERIES = 128
WIDTH = 768
MATES = (8, 12, 4)
LEAVES = (-3, -2, -1, 1, 2, 3)
HALVES = (pl.ds(0, WIDTH // 2), pl.ds(WIDTH // 2, WIDTH // 2))
SHIFTS = tuple((dy, dx) for dy in range(4) for dx in range(4) if (dy, dx) != (0, 0))


def inside(h):
    return (h >= 0) & (h < GROUPS)


def feeds(hub, o, core):
    if o == -1:
        return hub >= 1
    if o == 1:
        return hub <= 14
    if o == -3:
        return hub == 3
    if o == 3:
        return hub == 12
    if o == -2:
        return ((core == 0) & (hub >= 2)) | (hub == 2) | (hub == 3)
    return ((core == 1) & (hub <= 13)) | (hub == 12) | (hub == 13)


def hub_offsets(z, core):
    second = jnp.where(core == 0, jnp.where(z >= 14, -2, 2), jnp.where(z <= 1, 2, -2))
    return jnp.where(z == 15, -3, 1), jnp.where(z == 0, 3, -1), second


def place(h):
    return (h % 4) * 4 + h // 4


def rows_of(index, count=1):
    return pl.ds(pl.multiple_of(index * ROWS, ROWS), count * ROWS)


def score(a, b):
    return SCALE * lax.dot_general(
        a, b, (((1,), (1,)), ((), ())), preferred_element_type=jnp.float32
    )


def over_rows(a, b):
    return lax.dot_general(a, b, (((0,), (0,)), ((), ())), preferred_element_type=jnp.float32)


def dot(a, b):
    return jnp.dot(a, b, preferred_element_type=jnp.float32)


def kernel(
    q_in, p_in, pos_in, lists_in, counts_in,
    dq_out, dp_out, loss_out,
    lists, counts, q_buf, pos_own, pos_sib, p_buf, o_buf, s_buf, so_buf, g_buf, go_buf,
    st_mine, st_sib, dq_mine, dq_send, dq_sib,
    d_buf, r_buf, do_buf, leaf_buf, hub_buf, sum_buf, relay_buf, far_buf, acc,
    loc_sem, line_recv, hub_send, wide_send, wide_recv, leaf_send, far_send, far_recv, plane_send, plane_recv,
    sib_send, sib_recv, d_send, d_recv, leaf_send2, leaf_recv2, hub_send2, hub_recv2,
    relay_send2, relay_recv2, far_send2, far_recv2,
):
    g = lax.axis_index("grp")
    d = lax.axis_index("dp")
    y, zh, x, c = d // 16, (d // 8) % 2, (d // 2) % 4, d % 2

    def at(yy, zz, xx, cc):
        return ((yy * 2 + zz) * 4 + xx) * 2 + cc

    def mate(m):
        a = g // 4
        if m == 4:
            b = a + 1 - 2 * (a % 2)
        elif m == 8:
            b = (a + 2) % 4
        else:
            b = 3 - a
        return b * 4 + g % 4

    sib = (g, at(y, zh, x, 1 - c))
    plane = [(g, at((y + dy) % 4, zh, (x + dx) % 4, c)) for dy, dx in SHIFTS]
    far = (mate(8), at(y, 1 - zh, x, c))
    my_slot = y * 4 + x
    home = place(g)
    family = (g % 4) * 4

    def copy(src, dst, send, recv, dev):
        return pltpu.make_async_remote_copy(
            src_ref=src, dst_ref=dst, send_sem=send, recv_sem=recv,
            device_id=dev, device_id_type=MESH,
        )

    def received(dst, sem):
        copy(dst, dst, sem, sem, sib).wait_recv()

    barrier = pltpu.get_barrier_semaphore()

    def tell(dev):
        pl.semaphore_signal(barrier, inc=1, device_id=dev, device_id_type=MESH)

    tell((mate(8), d))
    tell(far)
    tell((mate(4), d))
    expected = jnp.int32(4 + len(SHIFTS))
    for o in LEAVES:
        pair = inside(g + o) & (feeds(g, o, c) | feeds(g + o, -o, c))
        pl.when(pair)(lambda o=o: tell((g + o, d)))
        expected = expected + pair.astype(jnp.int32)
    for dev in plane:
        tell(dev)
    tell(sib)

    own = p_buf.at[rows_of(my_slot)]
    local = [
        pltpu.make_async_copy(p_in, own, loc_sem.at[0]),
        pltpu.make_async_copy(p_in, o_buf.at[rows_of(home)], loc_sem.at[1]),
        pltpu.make_async_copy(q_in, q_buf.at[pl.ds(0, QUERIES)], loc_sem.at[2]),
        pltpu.make_async_copy(pos_in, pos_own, loc_sem.at[3]),
        pltpu.make_async_copy(lists_in, lists, loc_sem.at[4]),
        pltpu.make_async_copy(counts_in, counts, loc_sem.at[5]),
    ]
    for cp in local:
        cp.start()
    for cp in local:
        cp.wait()
    pl.semaphore_wait(barrier, expected)

    mine = o_buf.at[rows_of(home)]

    hub_copy = copy(mine, mine, hub_send.at[0], line_recv.at[home], (mate(4), d))

    def wide_copy(h):
        block = o_buf.at[rows_of(home), HALVES[h]]
        return copy(block, block, wide_send.at[h], wide_recv.at[h], (mate(8), d))

    other = place(mate(8))
    pass_copy = copy(
        o_buf.at[rows_of(other)], o_buf.at[rows_of(other)], hub_send.at[1], line_recv.at[other],
        (mate(4), d),
    )

    def leaf_copy(i, j, slot):
        block = o_buf.at[rows_of(slot)]
        return copy(block, block, leaf_send.at[i, j], line_recv.at[slot], (g + LEAVES[j], d))

    def leaf_each(act):
        for j, o in enumerate(LEAVES):
            pl.when(feeds(g, o, c) & inside(g + o))(lambda j=j: act(j))

    far_slot = 16 + my_slot

    def far_copy(h):
        return copy(
            o_buf.at[rows_of(other), HALVES[h]], p_buf.at[rows_of(far_slot), HALVES[h]],
            far_send.at[h], far_recv.at[h], far,
        )

    def plane_copy(i):
        return copy(own, own, plane_send.at[2, i], plane_recv.at[2, i], plane[i])

    def plane_copy2(h, i):
        block = p_buf.at[rows_of(far_slot), HALVES[h]]
        return copy(block, block, plane_send.at[h, i], plane_recv.at[h, i], plane[i])

    wide_copy(0).start()
    wide_copy(1).start()
    hub_copy.start()
    for i in range(15):
        plane_copy(i).start()
    leaf_each(lambda j: leaf_copy(3, j, home).start())
    q_copy = copy(
        q_buf.at[pl.ds(0, QUERIES)], q_buf.at[pl.ds(QUERIES, QUERIES)],
        sib_send.at[0], sib_recv.at[0], sib,
    )
    pos_copy = copy(pos_own, pos_sib, sib_send.at[1], sib_recv.at[1], sib)
    q_copy.start()
    pos_copy.start()

    for i in (0, 2, 1):
        slot = place(mate(MATES[i]))
        if MATES[i] == 8:
            for h in range(2):
                wide_copy(h).wait_recv()
                far_copy(h).start()
            pass_copy.start()
        else:
            received(o_buf.at[rows_of(slot)], line_recv.at[slot])
        leaf_each(lambda j, i=i, slot=slot: leaf_copy(i, j, slot).start())

    q_copy.wait_recv()
    pos_copy.wait_recv()
    pos = jnp.concatenate([pos_own[...], pos_sib[...]], axis=1)

    def hits(part):
        i = lax.broadcasted_iota(jnp.int32, (256, 2 * QUERIES), 0)
        zz = zh + part - 2 * zh * part
        column = ((i >> 6) << 8) + zz * 128 + (((i >> 4) & 3) << 5) + c * 16 + (i & 15)
        return column == pos

    def part_score(part):
        s = score(p_buf[part * 256 : part * 256 + 256], q_buf[...])
        s_buf[part * 256 : part * 256 + 256] = s
        top = jnp.max(s, axis=0, keepdims=True)
        total = jnp.sum(jnp.exp(s - top), axis=0, keepdims=True)
        picked = jnp.sum(jnp.where(hits(part), s, 0.0), axis=0, keepdims=True)
        return top, total, picked

    def join(a, b):
        top = jnp.maximum(a[0], b[0])
        return top, a[1] * jnp.exp(a[0] - top) + b[1] * jnp.exp(b[0] - top)

    for i in range(15):
        plane_copy(i).wait_recv()
    top0, total0, picked0 = part_score(0)

    for h in range(2):
        far_copy(h).wait_recv()
        for i in range(15):
            plane_copy2(h, i).start()

    for o in (1, 2, 3):
        for r in range(4):
            slot = ((g + o) % 4) * 4 + r
            received(o_buf.at[rows_of(slot)], line_recv.at[slot])
    row = lax.broadcasted_iota(jnp.int32, (GROUPS * ROWS, QUERIES), 0)
    row_group = ((row >> 4) & 3) * 4 + (row >> 6)
    live = jnp.zeros((GROUPS * ROWS, QUERIES), jnp.bool_)
    for i in range(4):
        entry = jnp.where(i < counts[0, 0], lists[0, i], -1)
        live = live | (row_group == entry)
    outer = jnp.where(live, score(o_buf[...], q_buf[0:QUERIES]), DEAD)
    so_buf[...] = outer
    outer_max = jnp.max(outer, axis=0, keepdims=True)
    outer_sum = jnp.sum(jnp.exp(outer - outer_max), axis=0, keepdims=True)
    half = join((top0[:, :QUERIES], total0[:, :QUERIES]), (outer_max, outer_sum))
    top0 = jnp.concatenate([half[0], top0[:, QUERIES:]], axis=1)
    total0 = jnp.concatenate([half[1], total0[:, QUERIES:]], axis=1)

    for i in range(15):
        plane_copy2(0, i).wait_recv()
        plane_copy2(1, i).wait_recv()
    top1, total1, picked1 = part_score(1)
    top, total = join((top0, total0), (top1, total1))
    picked = picked0 + picked1
    st_mine[0:1] = top
    st_mine[1:2] = total
    st_mine[2:3] = picked
    st_mine[3:8] = jnp.zeros((5, 2 * QUERIES), jnp.float32)
    st_copy = copy(st_mine, st_sib, sib_send.at[2], sib_recv.at[2], sib)
    st_copy.start()

    hub_copy.wait_send()
    pass_copy.wait_send()
    for h in range(2):
        wide_copy(h).wait_send()
        far_copy(h).wait_send()
    for i in range(3):
        slot = place(mate(MATES[i]))
        leaf_each(lambda j, i=i, slot=slot: leaf_copy(i, j, slot).wait_send())
    leaf_each(lambda j: leaf_copy(3, j, home).wait_send())
    for i in range(15):
        plane_copy(i).wait_send()
        plane_copy2(0, i).wait_send()
        plane_copy2(1, i).wait_send()
    q_copy.wait_send()
    pos_copy.wait_send()

    st_copy.wait()
    swapped = jnp.concatenate([st_sib[:, QUERIES:], st_sib[:, :QUERIES]], axis=1)
    top, total = join((top, total), (swapped[0:1], swapped[1:2]))
    log_total = top + jnp.log(total)
    loss_out[...] = (log_total - (picked + swapped[2:3]))[:, :QUERIES]

    def part_grad(part):
        a = jnp.exp(s_buf[part * 256 : part * 256 + 256] - log_total)
        a = (a - hits(part).astype(jnp.float32)).astype(jnp.bfloat16)
        g_buf[part * 256 : part * 256 + 256] = a
        d_buf[part * 256 : part * 256 + 256] = (SCALE * dot(a, q_buf[...])).astype(jnp.bfloat16)

    def to_slot(i):
        dy, dx = SHIFTS[i]
        return ((y + dy) % 4) * 4 + (x + dx) % 4

    def d_copy(i):
        return copy(
            d_buf.at[rows_of(to_slot(i))], r_buf.at[0, i], d_send.at[2, i], d_recv.at[2, i],
            plane[i],
        )

    def d_copy2(h, i):
        return copy(
            d_buf.at[rows_of(16 + to_slot(i)), HALVES[h]], r_buf.at[1, i, pl.ds(0, ROWS), HALVES[h]],
            d_send.at[h, i], d_recv.at[h, i], plane[i],
        )

    hubs = hub_offsets(g, c)

    def leaf_back(j, h):
        to = g + hubs[j]
        return copy(
            do_buf.at[rows_of((to % 4) * 4, 4), HALVES[h]],
            leaf_buf.at[3 - hubs[j], pl.ds(0, 4 * ROWS), HALVES[h]],
            leaf_send2.at[j, h], leaf_recv2.at[3 - hubs[j], h], (to, d),
        )

    part_grad(1)
    for h in range(2):
        for i in range(15):
            d_copy2(h, i).start()
    a = jnp.where(live, jnp.exp(so_buf[...] - log_total[:, :QUERIES]), 0.0).astype(jnp.bfloat16)
    go_buf[...] = a
    do_buf[...] = (SCALE * dot(a, q_buf[0:QUERIES])).astype(jnp.bfloat16)
    for h in range(2):
        for j in range(3):
            leaf_back(j, h).start()
    part_grad(0)

    dq_send[...] = over_rows(g_buf[:, QUERIES:], p_buf[...])
    dq_copy = copy(dq_send, dq_sib, sib_send.at[3], sib_recv.at[3], sib)
    dq_copy.start()
    dq_mine[...] = over_rows(g_buf[:, :QUERIES], p_buf[...]) + over_rows(go_buf[...], o_buf[...])

    near_rows, wide_rows, far_rows = pl.ds(0, 32), pl.ds(32, 16), pl.ds(48, 16)

    def near_back(h):
        return copy(
            sum_buf.at[near_rows, HALVES[h]], hub_buf.at[near_rows, HALVES[h]],
            hub_send2.at[0, h], hub_recv2.at[0, h], (mate(4), d),
        )

    def wide_back(h):
        return copy(
            sum_buf.at[wide_rows, HALVES[h]], hub_buf.at[wide_rows, HALVES[h]],
            hub_send2.at[1, h], hub_recv2.at[1, h], (mate(8), d),
        )

    def relay_copy(h):
        return copy(
            sum_buf.at[far_rows, HALVES[h]], relay_buf.at[pl.ds(0, ROWS), HALVES[h]],
            relay_send2.at[h], relay_recv2.at[h], (mate(8), d),
        )

    def far_back(h):
        return copy(
            relay_buf.at[pl.ds(0, ROWS), HALVES[h]], far_buf.at[pl.ds(0, ROWS), HALVES[h]],
            far_send2.at[h], far_recv2.at[h], far,
        )

    def class_sum(m, cols):
        return acc[rows_of(place(mate(m)) - family), cols]

    for h, cols in enumerate(HALVES):
        acc[:, cols] = do_buf[rows_of(family, 4), cols].astype(jnp.float32)
        for o in LEAVES:

            @pl.when(feeds(g, o, c) & inside(g + o))
            def _(o=o, h=h, cols=cols):
                received(leaf_buf.at[o + 3, pl.ds(0, 4 * ROWS), cols], leaf_recv2.at[o + 3, h])
                acc[:, cols] += leaf_buf[o + 3, :, cols].astype(jnp.float32)

        sum_buf[0:16, cols] = class_sum(4, cols).astype(jnp.bfloat16)
        sum_buf[16:32, cols] = class_sum(12, cols).astype(jnp.bfloat16)
        near_back(h).start()
        total_far = d_buf[rows_of(far_slot), cols].astype(jnp.float32)
        for i in range(15):
            d_copy2(h, i).wait_recv()
            total_far = total_far + r_buf[1, i, :, cols].astype(jnp.float32)
        sum_buf[48:64, cols] = total_far.astype(jnp.bfloat16)
        relay_copy(h).start()

    for i in range(15):
        d_copy(i).start()

    for h, cols in enumerate(HALVES):
        near_back(h).wait_recv()
        sum_buf[32:48, cols] = (
            class_sum(8, cols) + hub_buf[16:32, cols].astype(jnp.float32)
        ).astype(jnp.bfloat16)
        wide_back(h).start()
        relay_copy(h).wait_recv()
        far_back(h).start()

    dq_copy.wait_recv()
    dq_out[...] = (SCALE * (dq_mine[...] + dq_sib[...])).astype(jnp.bfloat16)

    total_own = acc[rows_of(home - family)] + d_buf[rows_of(my_slot)].astype(jnp.float32)
    for i in range(15):
        d_copy(i).wait_recv()
        total_own = total_own + r_buf[0, i].astype(jnp.float32)
    for i in range(15):
        d_copy(i).wait_send()
        d_copy2(0, i).wait_send()
        d_copy2(1, i).wait_send()
    dq_copy.wait_send()
    for h in range(2):
        for j in range(3):
            leaf_back(j, h).wait_send()
        relay_copy(h).wait_send()
        near_back(h).wait_send()
        wide_back(h).wait_send()
    wide_back(0).wait_recv()
    wide_back(1).wait_recv()
    total_own = total_own + hub_buf[0:16].astype(jnp.float32) + hub_buf[32:48].astype(jnp.float32)
    for h in range(2):
        far_back(h).wait_send()
        far_back(h).wait_recv()
    dp_out[...] = (total_own + far_buf[...].astype(jnp.float32)).astype(jnp.bfloat16)


def per_device(query_emb, passage_emb, positives, hard_lists, hard_counts):
    bf16, f32, i32 = jnp.bfloat16, jnp.float32, jnp.int32
    dma = pltpu.SemaphoreType.DMA
    block = (ROWS, WIDTH)
    hbm = pl.BlockSpec(memory_space=pltpu.HBM)
    vmem = pl.BlockSpec(memory_space=pltpu.VMEM)
    dq, dp, loss = pl.pallas_call(
        kernel,
        out_shape=(
            jax.ShapeDtypeStruct((QUERIES, WIDTH), bf16),
            jax.ShapeDtypeStruct(block, bf16),
            jax.ShapeDtypeStruct((1, QUERIES), f32),
        ),
        in_specs=[hbm] * 5,
        out_specs=(vmem, vmem, vmem),
        scratch_shapes=[
            pltpu.SMEM((1, 4), i32),
            pltpu.SMEM((1, 1), i32),
            pltpu.VMEM((2 * QUERIES, WIDTH), bf16),
            pltpu.VMEM((1, QUERIES), i32),
            pltpu.VMEM((1, QUERIES), i32),
            pltpu.VMEM((512, WIDTH), bf16),
            pltpu.VMEM((256, WIDTH), bf16),
            pltpu.VMEM((512, 2 * QUERIES), f32),
            pltpu.VMEM((256, QUERIES), f32),
            pltpu.VMEM((512, 2 * QUERIES), bf16),
            pltpu.VMEM((256, QUERIES), bf16),
            pltpu.VMEM((8, 2 * QUERIES), f32),
            pltpu.VMEM((8, 2 * QUERIES), f32),
            pltpu.VMEM((QUERIES, WIDTH), f32),
            pltpu.VMEM((QUERIES, WIDTH), f32),
            pltpu.VMEM((QUERIES, WIDTH), f32),
            pltpu.VMEM((512, WIDTH), bf16),
            pltpu.VMEM((2, 15) + block, bf16),
            pltpu.VMEM((256, WIDTH), bf16),
            pltpu.VMEM((7, 4 * ROWS, WIDTH), bf16),
            pltpu.VMEM((3 * ROWS, WIDTH), bf16),
            pltpu.VMEM((4 * ROWS, WIDTH), bf16),
            pltpu.VMEM(block, bf16),
            pltpu.VMEM(block, bf16),
            pltpu.VMEM((4 * ROWS, WIDTH), f32),
            dma((6,)),
            dma((16,)),
            dma((2,)),
            dma((2,)),
            dma((2,)),
            dma((4, 6)),
            dma((2,)),
            dma((2,)),
            dma((3, 15)),
            dma((3, 15)),
            dma((4,)),
            dma((4,)),
            dma((3, 15)),
            dma((3, 15)),
            dma((3, 2)),
            dma((7, 2)),
            dma((2, 2)),
            dma((2, 2)),
            dma((2,)),
            dma((2,)),
            dma((2,)),
            dma((2,)),
        ],
        name="dual_encoder",
        compiler_params=pltpu.CompilerParams(
            collective_id=0, has_side_effects=True, vmem_limit_bytes=60 * 1024 * 1024
        ),
    )(
        query_emb, passage_emb, positives.reshape(1, QUERIES), hard_lists.reshape(1, 4),
        hard_counts,
    )
    return dq, dp, loss.reshape(QUERIES)


def solution(mesh):
    in_specs = (
        P(("grp", "dp"), None),
        P(("grp", "dp"), None),
        P(("grp", "dp")),
        P("grp", "dp", None),
        P("grp", "dp"),
    )
    out_specs = (P(("grp", "dp"), None), P(("grp", "dp"), None), P(("grp", "dp")))
    return jax.shard_map(
        per_device, mesh=mesh, in_specs=in_specs, out_specs=out_specs, check_vma=False
    )
```

```python
import jax
import jax.numpy as jnp
from jax import lax
from jax.experimental import pallas as pl
from jax.experimental.pallas import tpu as pltpu
from jax.sharding import PartitionSpec as P

MESH = pl.DeviceIdType.MESH
SCALE = 20.0
DEAD = -1e30
GROUPS = 16
ROWS = 16
QUERIES = 128
WIDTH = 768
MATES = (8, 12, 4)
LEAVES = (-3, -2, -1, 1, 2, 3)
HALVES = (pl.ds(0, WIDTH // 2), pl.ds(WIDTH // 2, WIDTH // 2))
SHIFTS = tuple((dy, dx) for dy in range(4) for dx in range(4) if (dy, dx) != (0, 0))


def inside(h):
    return (h >= 0) & (h < GROUPS)


def feeds(hub, o, core):
    if o == -1:
        return hub >= 1
    if o == 1:
        return hub <= 14
    if o == -3:
        return hub == 3
    if o == 3:
        return hub == 12
    if o == -2:
        return ((core == 0) & (hub >= 2)) | (hub == 2) | (hub == 3)
    return ((core == 1) & (hub <= 13)) | (hub == 12) | (hub == 13)


def hub_offsets(z, core):
    second = jnp.where(core == 0, jnp.where(z >= 14, -2, 2), jnp.where(z <= 1, 2, -2))
    return jnp.where(z == 15, -3, 1), jnp.where(z == 0, 3, -1), second


def place(h):
    return (h % 4) * 4 + h // 4


def rows_of(index, count=1):
    return pl.ds(pl.multiple_of(index * ROWS, ROWS), count * ROWS)


def score(a, b):
    return SCALE * lax.dot_general(
        a, b, (((1,), (1,)), ((), ())), preferred_element_type=jnp.float32
    )


def over_rows(a, b):
    return lax.dot_general(a, b, (((0,), (0,)), ((), ())), preferred_element_type=jnp.float32)


def dot(a, b):
    return jnp.dot(a, b, preferred_element_type=jnp.float32)


def kernel(
    q_in, p_in, pos_in, lists_in, counts_in,
    dq_out, dp_out, loss_out,
    lists, counts, q_buf, pos_own, pos_sib, p_buf, o_buf, s_buf, so_buf, g_buf, go_buf,
    st_mine, st_sib, dq_mine, dq_send, dq_sib,
    d_buf, r_buf, do_buf, leaf_buf, hub_buf, sum_buf, relay_buf, far_buf, acc,
    loc_sem, line_recv, hub_send, wide_send, wide_recv, leaf_send, far_send, far_recv, plane_send, plane_recv,
    sib_send, sib_recv, d_send, d_recv, leaf_send2, leaf_recv2, hub_send2, hub_recv2,
    relay_send2, relay_recv2, far_send2, far_recv2,
):
    g = lax.axis_index("grp")
    d = lax.axis_index("dp")
    y, zh, x, c = d // 16, (d // 8) % 2, (d // 2) % 4, d % 2

    def at(yy, zz, xx, cc):
        return ((yy * 2 + zz) * 4 + xx) * 2 + cc

    def mate(m):
        a = g // 4
        if m == 4:
            b = a + 1 - 2 * (a % 2)
        elif m == 8:
            b = (a + 2) % 4
        else:
            b = 3 - a
        return b * 4 + g % 4

    sib = (g, at(y, zh, x, 1 - c))
    plane = [(g, at((y + dy) % 4, zh, (x + dx) % 4, c)) for dy, dx in SHIFTS]
    far = (mate(8), at(y, 1 - zh, x, c))
    my_slot = y * 4 + x
    home = place(g)
    family = (g % 4) * 4

    def copy(src, dst, send, recv, dev):
        return pltpu.make_async_remote_copy(
            src_ref=src, dst_ref=dst, send_sem=send, recv_sem=recv,
            device_id=dev, device_id_type=MESH,
        )

    def received(dst, sem):
        copy(dst, dst, sem, sem, sib).wait_recv()

    barrier = pltpu.get_barrier_semaphore()

    def tell(dev):
        pl.semaphore_signal(barrier, inc=1, device_id=dev, device_id_type=MESH)

    tell((mate(8), d))
    tell(far)
    tell((mate(4), d))
    expected = jnp.int32(4 + len(SHIFTS))
    for o in LEAVES:
        pair = inside(g + o) & (feeds(g, o, c) | feeds(g + o, -o, c))
        pl.when(pair)(lambda o=o: tell((g + o, d)))
        expected = expected + pair.astype(jnp.int32)
    for dev in plane:
        tell(dev)
    tell(sib)

    own = p_buf.at[rows_of(my_slot)]
    local = [
        pltpu.make_async_copy(p_in, own, loc_sem.at[0]),
        pltpu.make_async_copy(p_in, o_buf.at[rows_of(home)], loc_sem.at[1]),
        pltpu.make_async_copy(q_in, q_buf.at[pl.ds(0, QUERIES)], loc_sem.at[2]),
        pltpu.make_async_copy(pos_in, pos_own, loc_sem.at[3]),
        pltpu.make_async_copy(lists_in, lists, loc_sem.at[4]),
        pltpu.make_async_copy(counts_in, counts, loc_sem.at[5]),
    ]
    for cp in local:
        cp.start()
    for cp in local:
        cp.wait()
    pl.semaphore_wait(barrier, expected)

    mine = o_buf.at[rows_of(home)]

    hub_copy = copy(mine, mine, hub_send.at[0], line_recv.at[home], (mate(4), d))

    def wide_copy(h):
        block = o_buf.at[rows_of(home), HALVES[h]]
        return copy(block, block, wide_send.at[h], wide_recv.at[h], (mate(8), d))

    other = place(mate(8))
    pass_copy = copy(
        o_buf.at[rows_of(other)], o_buf.at[rows_of(other)], hub_send.at[1], line_recv.at[other],
        (mate(4), d),
    )

    def leaf_copy(i, j, slot):
        block = o_buf.at[rows_of(slot)]
        return copy(block, block, leaf_send.at[i, j], line_recv.at[slot], (g + LEAVES[j], d))

    def leaf_each(act):
        for j, o in enumerate(LEAVES):
            pl.when(feeds(g, o, c) & inside(g + o))(lambda j=j: act(j))

    far_slot = 16 + my_slot

    def far_copy(h):
        return copy(
            o_buf.at[rows_of(other), HALVES[h]], p_buf.at[rows_of(far_slot), HALVES[h]],
            far_send.at[h], far_recv.at[h], far,
        )

    def plane_copy(i):
        return copy(own, own, plane_send.at[2, i], plane_recv.at[2, i], plane[i])

    def plane_copy2(h, i):
        block = p_buf.at[rows_of(far_slot), HALVES[h]]
        return copy(block, block, plane_send.at[h, i], plane_recv.at[h, i], plane[i])

    wide_copy(0).start()
    wide_copy(1).start()
    hub_copy.start()
    for i in range(15):
        plane_copy(i).start()
    leaf_each(lambda j: leaf_copy(3, j, home).start())
    q_copy = copy(
        q_buf.at[pl.ds(0, QUERIES)], q_buf.at[pl.ds(QUERIES, QUERIES)],
        sib_send.at[0], sib_recv.at[0], sib,
    )
    pos_copy = copy(pos_own, pos_sib, sib_send.at[1], sib_recv.at[1], sib)
    q_copy.start()
    pos_copy.start()

    for i in (0, 2, 1):
        slot = place(mate(MATES[i]))
        if MATES[i] == 8:
            for h in range(2):
                wide_copy(h).wait_recv()
                far_copy(h).start()
            pass_copy.start()
        else:
            received(o_buf.at[rows_of(slot)], line_recv.at[slot])
        leaf_each(lambda j, i=i, slot=slot: leaf_copy(i, j, slot).start())

    q_copy.wait_recv()
    pos_copy.wait_recv()
    pos = jnp.concatenate([pos_own[...], pos_sib[...]], axis=1)

    def hits(part):
        i = lax.broadcasted_iota(jnp.int32, (256, 2 * QUERIES), 0)
        zz = zh + part - 2 * zh * part
        column = ((i >> 6) << 8) + zz * 128 + (((i >> 4) & 3) << 5) + c * 16 + (i & 15)
        return column == pos

    def part_score(part):
        s = score(p_buf[part * 256 : part * 256 + 256], q_buf[...])
        s_buf[part * 256 : part * 256 + 256] = s
        top = jnp.max(s, axis=0, keepdims=True)
        total = jnp.sum(jnp.exp(s - top), axis=0, keepdims=True)
        picked = jnp.sum(jnp.where(hits(part), s, 0.0), axis=0, keepdims=True)
        return top, total, picked

    def join(a, b):
        top = jnp.maximum(a[0], b[0])
        return top, a[1] * jnp.exp(a[0] - top) + b[1] * jnp.exp(b[0] - top)

    for i in range(15):
        plane_copy(i).wait_recv()
    top0, total0, picked0 = part_score(0)

    for h in range(2):
        far_copy(h).wait_recv()
        for i in range(15):
            plane_copy2(h, i).start()

    for o in (1, 2, 3):
        for r in range(4):
            slot = ((g + o) % 4) * 4 + r
            received(o_buf.at[rows_of(slot)], line_recv.at[slot])
    row = lax.broadcasted_iota(jnp.int32, (GROUPS * ROWS, QUERIES), 0)
    row_group = ((row >> 4) & 3) * 4 + (row >> 6)
    live = jnp.zeros((GROUPS * ROWS, QUERIES), jnp.bool_)
    for i in range(4):
        entry = jnp.where(i < counts[0, 0], lists[0, i], -1)
        live = live | (row_group == entry)
    outer = jnp.where(live, score(o_buf[...], q_buf[0:QUERIES]), DEAD)
    so_buf[...] = outer
    outer_max = jnp.max(outer, axis=0, keepdims=True)
    outer_sum = jnp.sum(jnp.exp(outer - outer_max), axis=0, keepdims=True)
    half = join((top0[:, :QUERIES], total0[:, :QUERIES]), (outer_max, outer_sum))
    top0 = jnp.concatenate([half[0], top0[:, QUERIES:]], axis=1)
    total0 = jnp.concatenate([half[1], total0[:, QUERIES:]], axis=1)

    for i in range(15):
        plane_copy2(0, i).wait_recv()
        plane_copy2(1, i).wait_recv()
    top1, total1, picked1 = part_score(1)
    top, total = join((top0, total0), (top1, total1))
    picked = picked0 + picked1
    st_mine[0:1] = top
    st_mine[1:2] = total
    st_mine[2:3] = picked
    st_mine[3:8] = jnp.zeros((5, 2 * QUERIES), jnp.float32)
    st_copy = copy(st_mine, st_sib, sib_send.at[2], sib_recv.at[2], sib)
    st_copy.start()

    hub_copy.wait_send()
    pass_copy.wait_send()
    for h in range(2):
        wide_copy(h).wait_send()
        far_copy(h).wait_send()
    for i in range(3):
        slot = place(mate(MATES[i]))
        leaf_each(lambda j, i=i, slot=slot: leaf_copy(i, j, slot).wait_send())
    leaf_each(lambda j: leaf_copy(3, j, home).wait_send())
    for i in range(15):
        plane_copy(i).wait_send()
        plane_copy2(0, i).wait_send()
        plane_copy2(1, i).wait_send()
    q_copy.wait_send()
    pos_copy.wait_send()

    st_copy.wait()
    swapped = jnp.concatenate([st_sib[:, QUERIES:], st_sib[:, :QUERIES]], axis=1)
    top, total = join((top, total), (swapped[0:1], swapped[1:2]))
    log_total = top + jnp.log(total)
    loss_out[...] = (log_total - (picked + swapped[2:3]))[:, :QUERIES]

    def part_grad(part):
        a = jnp.exp(s_buf[part * 256 : part * 256 + 256] - log_total)
        a = (a - hits(part).astype(jnp.float32)).astype(jnp.bfloat16)
        g_buf[part * 256 : part * 256 + 256] = a
        d_buf[part * 256 : part * 256 + 256] = (SCALE * dot(a, q_buf[...])).astype(jnp.bfloat16)

    def to_slot(i):
        dy, dx = SHIFTS[i]
        return ((y + dy) % 4) * 4 + (x + dx) % 4

    def d_copy(i):
        return copy(
            d_buf.at[rows_of(to_slot(i))], r_buf.at[0, i], d_send.at[2, i], d_recv.at[2, i],
            plane[i],
        )

    def d_copy2(h, i):
        return copy(
            d_buf.at[rows_of(16 + to_slot(i)), HALVES[h]], r_buf.at[1, i, pl.ds(0, ROWS), HALVES[h]],
            d_send.at[h, i], d_recv.at[h, i], plane[i],
        )

    hubs = hub_offsets(g, c)

    def leaf_back(j, h):
        to = g + hubs[j]
        return copy(
            do_buf.at[rows_of((to % 4) * 4, 4), HALVES[h]],
            leaf_buf.at[3 - hubs[j], pl.ds(0, 4 * ROWS), HALVES[h]],
            leaf_send2.at[j, h], leaf_recv2.at[3 - hubs[j], h], (to, d),
        )

    a = jnp.where(live, jnp.exp(so_buf[...] - log_total[:, :QUERIES]), 0.0).astype(jnp.bfloat16)
    go_buf[...] = a
    do_buf[...] = (SCALE * dot(a, q_buf[0:QUERIES])).astype(jnp.bfloat16)
    for h in range(2):
        for j in range(3):
            leaf_back(j, h).start()
    part_grad(1)
    for h in range(2):
        for i in range(15):
            d_copy2(h, i).start()
    part_grad(0)

    dq_send[...] = over_rows(g_buf[:, QUERIES:], p_buf[...])
    dq_copy = copy(dq_send, dq_sib, sib_send.at[3], sib_recv.at[3], sib)
    dq_copy.start()
    dq_mine[...] = over_rows(g_buf[:, :QUERIES], p_buf[...]) + over_rows(go_buf[...], o_buf[...])

    near_rows, wide_rows, far_rows = pl.ds(0, 32), pl.ds(32, 16), pl.ds(48, 16)

    def near_back(h):
        return copy(
            sum_buf.at[near_rows, HALVES[h]], hub_buf.at[near_rows, HALVES[h]],
            hub_send2.at[0, h], hub_recv2.at[0, h], (mate(4), d),
        )

    def wide_back(h):
        return copy(
            sum_buf.at[wide_rows, HALVES[h]], hub_buf.at[wide_rows, HALVES[h]],
            hub_send2.at[1, h], hub_recv2.at[1, h], (mate(8), d),
        )

    def relay_copy(h):
        return copy(
            sum_buf.at[far_rows, HALVES[h]], relay_buf.at[pl.ds(0, ROWS), HALVES[h]],
            relay_send2.at[h], relay_recv2.at[h], (mate(8), d),
        )

    def far_back(h):
        return copy(
            relay_buf.at[pl.ds(0, ROWS), HALVES[h]], far_buf.at[pl.ds(0, ROWS), HALVES[h]],
            far_send2.at[h], far_recv2.at[h], far,
        )

    def class_sum(m, cols):
        return acc[rows_of(place(mate(m)) - family), cols]

    for h, cols in enumerate(HALVES):
        acc[:, cols] = do_buf[rows_of(family, 4), cols].astype(jnp.float32)
        for o in LEAVES:

            @pl.when(feeds(g, o, c) & inside(g + o))
            def _(o=o, h=h, cols=cols):
                received(leaf_buf.at[o + 3, pl.ds(0, 4 * ROWS), cols], leaf_recv2.at[o + 3, h])
                acc[:, cols] += leaf_buf[o + 3, :, cols].astype(jnp.float32)

        sum_buf[0:16, cols] = class_sum(4, cols).astype(jnp.bfloat16)
        sum_buf[16:32, cols] = class_sum(12, cols).astype(jnp.bfloat16)
        near_back(h).start()
        total_far = d_buf[rows_of(far_slot), cols].astype(jnp.float32)
        for i in range(15):
            d_copy2(h, i).wait_recv()
            total_far = total_far + r_buf[1, i, :, cols].astype(jnp.float32)
        sum_buf[48:64, cols] = total_far.astype(jnp.bfloat16)
        relay_copy(h).start()

    for i in range(15):
        d_copy(i).start()

    for h, cols in enumerate(HALVES):
        near_back(h).wait_recv()
        sum_buf[32:48, cols] = (
            class_sum(8, cols) + hub_buf[16:32, cols].astype(jnp.float32)
        ).astype(jnp.bfloat16)
        wide_back(h).start()
        relay_copy(h).wait_recv()
        far_back(h).start()

    dq_copy.wait_recv()
    dq_out[...] = (SCALE * (dq_mine[...] + dq_sib[...])).astype(jnp.bfloat16)

    total_own = acc[rows_of(home - family)] + d_buf[rows_of(my_slot)].astype(jnp.float32)
    for i in range(15):
        d_copy(i).wait_recv()
        total_own = total_own + r_buf[0, i].astype(jnp.float32)
    for i in range(15):
        d_copy(i).wait_send()
        d_copy2(0, i).wait_send()
        d_copy2(1, i).wait_send()
    dq_copy.wait_send()
    for h in range(2):
        for j in range(3):
            leaf_back(j, h).wait_send()
        relay_copy(h).wait_send()
        near_back(h).wait_send()
        wide_back(h).wait_send()
    wide_back(0).wait_recv()
    wide_back(1).wait_recv()
    total_own = total_own + hub_buf[0:16].astype(jnp.float32) + hub_buf[32:48].astype(jnp.float32)
    for h in range(2):
        far_back(h).wait_send()
        far_back(h).wait_recv()
    dp_out[...] = (total_own + far_buf[...].astype(jnp.float32)).astype(jnp.bfloat16)


def per_device(query_emb, passage_emb, positives, hard_lists, hard_counts):
    bf16, f32, i32 = jnp.bfloat16, jnp.float32, jnp.int32
    dma = pltpu.SemaphoreType.DMA
    block = (ROWS, WIDTH)
    hbm = pl.BlockSpec(memory_space=pltpu.HBM)
    vmem = pl.BlockSpec(memory_space=pltpu.VMEM)
    dq, dp, loss = pl.pallas_call(
        kernel,
        out_shape=(
            jax.ShapeDtypeStruct((QUERIES, WIDTH), bf16),
            jax.ShapeDtypeStruct(block, bf16),
            jax.ShapeDtypeStruct((1, QUERIES), f32),
        ),
        in_specs=[hbm] * 5,
        out_specs=(vmem, vmem, vmem),
        scratch_shapes=[
            pltpu.SMEM((1, 4), i32),
            pltpu.SMEM((1, 1), i32),
            pltpu.VMEM((2 * QUERIES, WIDTH), bf16),
            pltpu.VMEM((1, QUERIES), i32),
            pltpu.VMEM((1, QUERIES), i32),
            pltpu.VMEM((512, WIDTH), bf16),
            pltpu.VMEM((256, WIDTH), bf16),
            pltpu.VMEM((512, 2 * QUERIES), f32),
            pltpu.VMEM((256, QUERIES), f32),
            pltpu.VMEM((512, 2 * QUERIES), bf16),
            pltpu.VMEM((256, QUERIES), bf16),
            pltpu.VMEM((8, 2 * QUERIES), f32),
            pltpu.VMEM((8, 2 * QUERIES), f32),
            pltpu.VMEM((QUERIES, WIDTH), f32),
            pltpu.VMEM((QUERIES, WIDTH), f32),
            pltpu.VMEM((QUERIES, WIDTH), f32),
            pltpu.VMEM((512, WIDTH), bf16),
            pltpu.VMEM((2, 15) + block, bf16),
            pltpu.VMEM((256, WIDTH), bf16),
            pltpu.VMEM((7, 4 * ROWS, WIDTH), bf16),
            pltpu.VMEM((3 * ROWS, WIDTH), bf16),
            pltpu.VMEM((4 * ROWS, WIDTH), bf16),
            pltpu.VMEM(block, bf16),
            pltpu.VMEM(block, bf16),
            pltpu.VMEM((4 * ROWS, WIDTH), f32),
            dma((6,)),
            dma((16,)),
            dma((2,)),
            dma((2,)),
            dma((2,)),
            dma((4, 6)),
            dma((2,)),
            dma((2,)),
            dma((3, 15)),
            dma((3, 15)),
            dma((4,)),
            dma((4,)),
            dma((3, 15)),
            dma((3, 15)),
            dma((3, 2)),
            dma((7, 2)),
            dma((2, 2)),
            dma((2, 2)),
            dma((2,)),
            dma((2,)),
            dma((2,)),
            dma((2,)),
        ],
        name="dual_encoder",
        compiler_params=pltpu.CompilerParams(
            collective_id=0, has_side_effects=True, vmem_limit_bytes=60 * 1024 * 1024
        ),
    )(
        query_emb, passage_emb, positives.reshape(1, QUERIES), hard_lists.reshape(1, 4),
        hard_counts,
    )
    return dq, dp, loss.reshape(QUERIES)


def solution(mesh):
    in_specs = (
        P(("grp", "dp"), None),
        P(("grp", "dp"), None),
        P(("grp", "dp")),
        P("grp", "dp", None),
        P("grp", "dp"),
    )
    out_specs = (P(("grp", "dp"), None), P(("grp", "dp"), None), P(("grp", "dp")))
    return jax.shard_map(
        per_device, mesh=mesh, in_specs=in_specs, out_specs=out_specs, check_vma=False
    )
```
